32 devices in a mesh: src: 8 (over y, x, core), rcv: 4 (over z).
Axes of the slice: x: 2, y: 2, z: 4, core: 2. Of those that a mesh axis runs over, the one named last changes fastest.
Arguments:
- recorded: bfloat16 [2, 16384, 16384], P(None, 'src', 'rcv'), may hold values from -6 to 6
- obliquity: float32 [4, 4096], replicated, may hold values from 0.01 to 0.25
- clip_level: float32 [16384], P('src'), may hold values from 0.3 to 3
Outputs:
- first_pass: bfloat16 [2, 16384, 16384], P(None, 'src', 'rcv')
- primaries: bfloat16 [2, 16384, 16384], P(None, 'src', 'rcv')
The draws below stay inside these ranges and needn't reach their ends.
All inputs are finite; a program needn't handle non-finite values.
Results may differ from the reference program's by a relative error of at most 0.0025.
Values may be sent and summed in bfloat16 or wider, within the bound.
No kernel may reach another device: no remote copies, remote signals or barrier semaphores. Data moves between devices by JAX's collectives and lax.ppermute only.
A program may use at most 576 MiB of HBM per device.

```python
import math
import jax
import jax.numpy as jnp
from jax import lax

N = 16384
K = 256
GROUPS = 4
COLS = 4096


def shard_levels(key, extent, split, smallest, largest):
    level, own = 1.0, jax.random.fold_in(key, 6)
    for position, shards_of in split:
        heights = jnp.exp(jax.random.uniform(jax.random.fold_in(own, position), (shards_of,), jnp.float32, smallest / len(split), largest / len(split)))
        level = level * jnp.repeat(heights, extent[position] // shards_of).reshape([-1 if axis == position else 1 for axis in range(len(extent))])
    return level


def gaussian(own_key, shape, spread, bound, pieces=(), kind=jnp.bfloat16):
    drawn = jax.random.normal(own_key, shape, jnp.float32) * spread
    if len(pieces) > 0:
        drawn = shard_levels(own_key, shape, pieces, -0.22, 0.18) * drawn
    return jnp.clip(drawn, min=-bound, max=bound).astype(kind)


def setup_inputs(seed: int = 0) -> dict:
    key_list = jax.random.split(jax.random.key(seed), 4)
    recorded = gaussian(key_list[0], (2, N, N), 1.0, 6.0, ((1, 8), (2, 4)))
    obliquity = jnp.clip(jnp.exp(jax.random.uniform(key_list[1], (GROUPS, COLS), jnp.float32, math.log(0.01), math.log(0.25))), 0.01, 0.25)
    clip_level = jnp.clip(jnp.exp(math.log(3.0) - 2.3025851 * jax.random.uniform(key_list[2], (N,), jnp.float32) ** shard_levels(key_list[2], (N,), ((0, 8),), -0.2, 0.2)), 0.3, 3.0)
    return dict(recorded=recorded, obliquity=obliquity, clip_level=clip_level)


def apply_update(left_columns, recorded, right_joined, clip_level):
    block_rows = min(1024, N)
    block_total = N // block_rows
    left_joined = jnp.concatenate([left_columns[0], left_columns[1]], axis=1).astype(jnp.float32)

    def one_block(block_index):
        first_row = block_index * block_rows
        left_rows = lax.dynamic_slice_in_dim(left_joined, first_row, block_rows, 0)
        product_sum = jnp.dot(left_rows, right_joined, precision=lax.Precision.HIGHEST, preferred_element_type=jnp.float32)
        pred_real = product_sum[:, :N]
        pred_imag = product_sum[:, N:]
        clip_rows = lax.dynamic_slice_in_dim(clip_level, first_row, block_rows, 0)[:, None]
        limiter = 1.0 / jnp.sqrt(1.0 + (pred_real * pred_real + pred_imag * pred_imag) / (clip_rows * clip_rows))
        base_rows = lax.dynamic_slice_in_dim(recorded, first_row, block_rows, 1).astype(jnp.float32)
        return (base_rows - jnp.stack([pred_real * limiter, pred_imag * limiter])).astype(jnp.bfloat16)
    blocks = lax.map(one_block, jnp.arange(block_total, dtype=jnp.int32))
    return jnp.transpose(blocks, (1, 0, 2, 3)).reshape(2, N, N)

def reference(recorded, obliquity, clip_level):
    spacing = N // K
    panel = recorded[:, ::spacing, :].astype(jnp.float32)
    spectrum = jnp.fft.fft(panel[0] + 1j * panel[1], axis=-1)
    weights = jnp.transpose(obliquity).reshape(-1)
    filtered_complex = jnp.fft.ifft(spectrum * weights, axis=-1)
    filtered = jnp.stack([jnp.real(filtered_complex), jnp.imag(filtered_complex)]).astype(jnp.bfloat16)
    filtered = lax.optimization_barrier(filtered).astype(jnp.float32)
    upper = jnp.concatenate([filtered[0], filtered[1]], axis=1)
    lower = jnp.concatenate([-filtered[1], filtered[0]], axis=1)
    right_joined = jnp.concatenate([upper, lower], axis=0)
    first_pass = apply_update(recorded[:, :, ::spacing], recorded, right_joined, clip_level)
    primaries = apply_update(first_pass[:, :, ::spacing], recorded, right_joined, clip_level)
    return (first_pass, primaries)
```

```python
import functools
import math

import jax
import jax.numpy as jnp
import numpy as np
from jax import lax
from jax.experimental import pallas as pl
from jax.experimental.pallas import tpu as pltpu
from jax.sharding import PartitionSpec as P

LANES = 128
PANEL = 256
BF16 = jnp.bfloat16
F32 = jnp.float32
VMEM_BYTES = 56 * 2**20


class Sizes:
    def __init__(self, recorded, n_src, n_rcv):
        self.n_src, self.n_rcv = n_src, n_rcv
        self.rows, self.cols = recorded.shape[1], recorded.shape[2]
        self.order = self.cols * n_rcv
        self.spacing = self.order // PANEL
        self.group = PANEL // n_src
        self.own = self.group // n_rcv
        self.panel_cols = PANEL // n_rcv
        self.slots = self.cols // LANES
        self.points = self.order // LANES
        self.halves = LANES // self.spacing
        self.depth = 2 * PANEL

    def fits(self):
        return (
            self.points == LANES
            and self.n_src & (self.n_src - 1) == 0
            and self.n_src > 2
            and self.group % self.n_rcv == 0
            and self.own % 8 == 0
            and self.panel_cols % self.group == 0
            and 2 * self.panel_cols == LANES
            and self.spacing % 16 == 0
            and self.halves * LANES == PANEL
            and self.rows % 256 == 0
        )


def transform_tables(points, order):
    index = np.arange(points)
    angles = np.outer(index, index) % points * (2.0 * math.pi / points)
    cosine, sine = np.cos(angles), np.sin(angles)
    table = np.block([[cosine, sine], [-sine, cosine]]).astype(np.float32)
    high = table.astype(BF16)
    low = (table - high.astype(np.float32)).astype(BF16)
    turns = np.outer(index, np.arange(LANES)) % order * (2.0 * math.pi / order)
    factors = np.stack([np.cos(turns), np.sin(turns)]).astype(np.float32)
    return np.stack([high, low, high.T, low.T]), factors


def lane_parts(lane, s):
    group, rest = lane // (2 * s.group), lane % (2 * s.group)
    owner, rest = rest // (2 * s.own), rest % (2 * s.own)
    part, row = rest // s.own, rest % s.own
    return group * s.group + owner * s.own + row, part


def pick_rows_kernel(s, recorded, *refs):
    outs, (held, lines, sems) = refs[: s.n_rcv], refs[s.n_rcv :]
    me = lax.axis_index("rcv")

    def copy(index):
        ahead, row = index // s.own, index % s.own
        line = lax.rem(me + ahead, s.n_rcv) * s.own + row
        first = pl.multiple_of(line * s.spacing, 16)
        return pltpu.make_async_copy(
            recorded.at[:, pl.ds(first, 16), :], held.at[index], sems.at[index]
        )

    for index in range(s.group):
        copy(index).start()
    for index in range(s.group):
        copy(index).wait()
        for part in range(2):
            line = held[index, part].astype(F32)[0:1]
            for slot in range(s.slots):
                lines[slot : slot + 1, :] = line[:, slot * LANES : (slot + 1) * LANES]
            outs[index // s.own][index % s.own, part] = lines[...].astype(BF16)


def pick_rows(recorded, s):
    shape = (s.own, 2, s.slots, LANES)
    return pl.pallas_call(
        functools.partial(pick_rows_kernel, s),
        in_specs=[pl.BlockSpec(memory_space=pl.ANY)],
        out_shape=[jax.ShapeDtypeStruct(shape, BF16)] * s.n_rcv,
        scratch_shapes=[
            pltpu.VMEM((s.group, 2, 16, s.cols), BF16),
            pltpu.VMEM((s.slots, LANES), F32),
            pltpu.SemaphoreType.DMA((s.group,)),
        ],
        compiler_params=pltpu.CompilerParams(vmem_limit_bytes=VMEM_BYTES),
        name="pick_rows",
    )(recorded)


def pick_columns_kernel(s, recorded, out, select):
    @pl.when(pl.program_id(0) == 0)
    def _():
        shape = (s.cols, LANES)
        receiver = lax.broadcasted_iota(jnp.int32, shape, 0)
        column, part = lane_parts(lax.broadcasted_iota(jnp.int32, shape, 1), s)
        for which in range(2):
            chosen = (receiver == column * s.spacing) & (part == which)
            select[which] = jnp.where(chosen, 1.0, 0.0).astype(BF16)

    real = jnp.dot(recorded[0], select[0], preferred_element_type=F32)
    imag = jnp.dot(recorded[1], select[1], preferred_element_type=F32)
    out[...] = (real + imag).astype(BF16)


def pick_columns(recorded, s):
    block = 256
    return pl.pallas_call(
        functools.partial(pick_columns_kernel, s),
        grid=(s.rows // block,),
        in_specs=[pl.BlockSpec((2, block, s.cols), lambda i: (0, i, 0))],
        out_specs=pl.BlockSpec((block, LANES), lambda i: (i, 0)),
        out_shape=jax.ShapeDtypeStruct((s.rows, LANES), BF16),
        scratch_shapes=[pltpu.VMEM((2, s.cols, LANES), BF16)],
        compiler_params=pltpu.CompilerParams(vmem_limit_bytes=VMEM_BYTES),
        name="pick_columns",
    )(recorded)


def split(values):
    high = values.astype(BF16)
    return high, (values - high.astype(F32)).astype(BF16)


def dot(left, right):
    return jnp.dot(left, right, preferred_element_type=F32)


def filter_kernel(s, *refs):
    blocks, refs = refs[: s.n_rcv], refs[s.n_rcv :]
    tables, factors, weights = refs[:3]
    outs = refs[3 : 3 + s.n_rcv]
    values, joined, turned, sorted_rows = refs[3 + s.n_rcv :]
    me = lax.axis_index("rcv")
    n = s.points
    lanes = [slice(r * LANES, (r + 1) * LANES) for r in range(s.own)]
    rows = [slice(r * n, (r + 1) * n) for r in range(s.own)]
    for behind in range(s.n_rcv):
        owner = lax.rem(me + s.n_rcv - behind, s.n_rcv)
        for part in range(2):
            place = pl.ds(pl.multiple_of(part * n + owner * s.slots, 16), s.slots)
            for r in range(s.own):
                values[place, lanes[r]] = blocks[behind][r, part]
    cosine, sine = factors[0], factors[1]
    first = dot(tables[0], values[...]) + dot(tables[1], values[...])
    for r in range(s.own):
        real, imag = first[:n, lanes[r]], first[n:, lanes[r]]
        joined[rows[r], :LANES] = real * cosine + imag * sine
        joined[rows[r], LANES:] = imag * cosine - real * sine
    high, low = split(joined[...])
    spectrum = dot(high, tables[2]) + (dot(high, tables[3]) + dot(low, tables[2]))
    scale = jnp.concatenate([weights[...], weights[...]], axis=1)
    for r in range(s.own):
        joined[rows[r], :] = spectrum[rows[r]] * scale
    high, low = split(joined[...])
    back = dot(high, tables[0]) + (dot(high, tables[1]) + dot(low, tables[0]))
    cosine, sine = cosine * (1.0 / s.order), sine * (1.0 / s.order)
    for r in range(s.own):
        real, imag = back[rows[r], :LANES], back[rows[r], LANES:]
        turned[:n, lanes[r]] = real * cosine - imag * sine
        turned[n:, lanes[r]] = real * sine + imag * cosine
    high, low = split(turned[...])
    result = dot(tables[2], high) + (dot(tables[3], high) + dot(tables[2], low))

    shape = (s.halves * s.own, s.own * LANES)
    wanted = lax.broadcasted_iota(jnp.int32, shape, 0)
    lane = lax.broadcasted_iota(jnp.int32, shape, 1)
    chosen = lane == (wanted % s.own) * LANES + (wanted // s.own) * s.spacing
    select = jnp.where(chosen, 1.0, 0.0).astype(BF16)
    rounded = result.astype(BF16)
    picked = [
        lax.dot_general(
            select,
            rounded[part * n : (part + 1) * n],
            (((1,), (1,)), ((), ())),
            preferred_element_type=F32,
        )
        for part in range(2)
    ]
    for half in range(s.halves):
        place = slice(half * s.own, (half + 1) * s.own)
        extra = jnp.concatenate([picked[0][place], picked[1][place]], axis=0).astype(BF16)
        for out in outs:
            out[s.slots + half] = extra

    height = 2 * s.own
    for part in range(2):
        for r in range(s.own):
            place = pl.ds(part * s.own + r, n, stride=height)
            sorted_rows[place, :] = result[part * n : (part + 1) * n, lanes[r]]
    for ahead in range(s.n_rcv):
        owner = lax.rem(me + ahead, s.n_rcv)
        first_row = pl.multiple_of(owner * s.slots * height, 16)
        mine = sorted_rows[pl.ds(first_row, s.slots * height), :]
        outs[ahead][: s.slots] = mine.reshape(s.slots, height, LANES).astype(BF16)


def filter_rows(blocks, obliquity, s):
    tables, factors = transform_tables(s.points, s.order)
    weights = jnp.transpose(jnp.transpose(obliquity).reshape(LANES, s.points))
    shape = (s.slots + s.halves, 2 * s.own, LANES)
    return pl.pallas_call(
        functools.partial(filter_kernel, s),
        out_shape=[jax.ShapeDtypeStruct(shape, BF16)] * s.n_rcv,
        scratch_shapes=[
            pltpu.VMEM((2 * s.points, s.own * LANES), BF16),
            pltpu.VMEM((s.own * s.points, 2 * LANES), F32),
            pltpu.VMEM((2 * s.points, s.own * LANES), F32),
            pltpu.VMEM((2 * s.own * s.points, LANES), F32),
        ],
        compiler_params=pltpu.CompilerParams(vmem_limit_bytes=VMEM_BYTES),
        name="filter_rows",
    )(*blocks, jnp.asarray(tables), jnp.asarray(factors), weights)


TWO_PI = 2.0 * math.pi


def turn(real_part, imag_part, cosine, sine_part):
    return (real_part * cosine - imag_part * sine_part, real_part * sine_part + imag_part * cosine)


def twiddle(real_part, imag_part, column_index, group_index, orient, total_length):
    angles = (column_index * group_index % total_length).astype(jnp.float32) * (
        TWO_PI / total_length
    )
    return turn(real_part, imag_part, jnp.cos(angles), orient * jnp.sin(angles))


def long_table(length, orient):
    index_left = lax.broadcasted_iota(jnp.int32, (length, length), 0)
    index_right = lax.broadcasted_iota(jnp.int32, (length, length), 1)
    angles = (index_left * index_right % length).astype(jnp.float32) * (TWO_PI / length)
    cosine = jnp.cos(angles)
    sine_part = orient * jnp.sin(angles)
    upper = jnp.concatenate([cosine, sine_part], axis=1)
    lower = jnp.concatenate([-sine_part, cosine], axis=1)
    return jnp.concatenate([upper, lower], axis=0)


def long_transform(real_part, imag_part, orient):
    length = real_part.shape[-1]
    joined = jnp.concatenate([real_part, imag_part], axis=-1)
    result = jnp.dot(
        joined.reshape(-1, 2 * length),
        long_table(length, orient),
        precision=lax.Precision.HIGHEST,
        preferred_element_type=jnp.float32,
    )
    result = result.reshape(joined.shape)
    return (result[..., :length], result[..., length:])


def across_groups(real_part, imag_part, groups, orient):
    index_left = lax.broadcasted_iota(jnp.int32, (groups, groups), 0)
    index_right = lax.broadcasted_iota(jnp.int32, (groups, groups), 1)
    angles = (index_left * index_right % groups).astype(jnp.float32) * (TWO_PI / groups)
    cosine = jnp.cos(angles)
    sine_part = orient * jnp.sin(angles)
    highest = lax.Precision.HIGHEST
    new_real = jnp.einsum("mgc,gk->mkc", real_part, cosine, precision=highest) - jnp.einsum(
        "mgc,gk->mkc", imag_part, sine_part, precision=highest
    )
    new_imag = jnp.einsum("mgc,gk->mkc", real_part, sine_part, precision=highest) + jnp.einsum(
        "mgc,gk->mkc", imag_part, cosine, precision=highest
    )
    return (new_real, new_imag)


def plain_filter(whole_rows, obliquity, groups):
    row_total = whole_rows.shape[1]
    group_cols = whole_rows.shape[2] // groups
    total_length = groups * group_cols
    values = whole_rows.astype(jnp.float32).reshape(2, row_total, groups, group_cols)
    real_part, imag_part = across_groups(values[0], values[1], groups, -1.0)
    column_index = lax.broadcasted_iota(jnp.int32, (1, 1, group_cols), 2)
    group_index = lax.broadcasted_iota(jnp.int32, (1, groups, 1), 1)
    real_part, imag_part = twiddle(
        real_part, imag_part, column_index, group_index, -1.0, total_length
    )
    real_part, imag_part = long_transform(real_part, imag_part, -1.0)
    real_part = real_part * obliquity[None]
    imag_part = imag_part * obliquity[None]
    real_part, imag_part = long_transform(real_part, imag_part, 1.0)
    real_part, imag_part = twiddle(
        real_part, imag_part, column_index, group_index, 1.0, total_length
    )
    real_part, imag_part = across_groups(real_part, imag_part, groups, 1.0)
    inverse_scale = 1.0 / total_length
    returned = jnp.stack([real_part * inverse_scale, imag_part * inverse_scale])
    return returned.reshape(2, row_total, total_length).astype(jnp.bfloat16)


def through_rows(panel_rows, obliquity):
    moved_rows = lax.all_to_all(panel_rows, "rcv", split_axis=1, concat_axis=2, tiled=True)
    returned = plain_filter(moved_rows, obliquity, lax.axis_size("rcv"))
    return lax.all_to_all(returned, "rcv", split_axis=2, concat_axis=1, tiled=True)


def complex_product(left_rows, right_rows):
    left_joined = jnp.concatenate([left_rows[0], left_rows[1]], axis=0)
    upper = jnp.concatenate([right_rows[0], right_rows[1]], axis=1)
    lower = jnp.concatenate([-right_rows[1], right_rows[0]], axis=1)
    right_joined = jnp.concatenate([upper, lower], axis=0)
    return lax.dot_general(
        left_joined, right_joined, (((0,), (0,)), ((), ())), preferred_element_type=jnp.float32
    )


def plain_device(recorded, obliquity, clip_level):
    spacing = recorded.shape[2] * lax.axis_size("rcv") // PANEL
    row_total = recorded.shape[1]
    col_total = recorded.shape[2]
    panel_rows = recorded.reshape(2, row_total // spacing, spacing, col_total)[:, :, 0, :]
    filtered = through_rows(panel_rows, obliquity)
    clip_rows = clip_level[:, None]
    estimate = recorded
    passes = []
    for update_index in range(2):
        columns = estimate.reshape(2, row_total, col_total // spacing, spacing)[:, :, :, 0]
        left_local = jnp.swapaxes(columns, 1, 2)
        left_panel = lax.all_gather(left_local, "rcv", axis=1, tiled=True)

        def accumulate(running, panel_piece, first_row, left_all=left_panel):
            return complex_product(left_all, panel_piece)

        zeros_init = jnp.zeros((row_total, 2 * col_total), jnp.float32)
        product_sum = accumulate(
            zeros_init, lax.all_gather(filtered, "src", axis=1, tiled=True), jnp.int32(0)
        )
        pred_real = product_sum[:, :col_total]
        pred_imag = product_sum[:, col_total:]
        limiter = lax.rsqrt(
            1.0 + (pred_real * pred_real + pred_imag * pred_imag) / (clip_rows * clip_rows)
        )
        estimate = (
            recorded.astype(jnp.float32) - jnp.stack([pred_real * limiter, pred_imag * limiter])
        ).astype(jnp.bfloat16)
        passes.append(estimate)
    return (passes[0], passes[1])


def limited(real, imag, clip, clip_squared):
    return clip * lax.rsqrt(clip_squared + (real * real + imag * imag))


def update_kernel(s, tile_rows, tile_slots, *refs):
    count = 2 * s.n_rcv - 1
    recorded, clip_rows = refs[:2]
    left_blocks, refs = refs[2 : 2 + count], refs[2 + count :]
    filtered, refs = refs[: s.n_src * s.n_rcv], refs[s.n_src * s.n_rcv :]
    out_first, out_second, right, own_columns, left, sems = refs
    src, rcv = lax.axis_index("src"), lax.axis_index("rcv")
    width = tile_slots * LANES

    @pl.when(pl.program_id(0) == 0)
    def _():
        copies = []
        for across in range(s.n_src):
            for behind in range(s.n_rcv):
                index = across * s.n_rcv + behind
                owner = lax.rem(rcv + s.n_rcv - behind, s.n_rcv)
                place = (src ^ across) * s.n_rcv + owner
                copies.append(
                    pltpu.make_async_copy(filtered[index], right.at[place], sems.at[index])
                )
        for copy in copies:
            copy.start()
        for copy in copies:
            copy.wait()
        row = lax.broadcasted_iota(jnp.int32, (PANEL, s.depth), 0)
        lane = lax.broadcasted_iota(jnp.int32, (PANEL, s.depth), 1)
        column, _part = lane_parts(lane % LANES, s)
        column = column + (lane // LANES) * s.panel_cols
        chosen = row == (column % s.halves) * LANES + column // s.halves
        spread = jnp.where(chosen, 1.0, 0.0).astype(BF16)
        held = [right[:, s.slots + h].reshape(s.depth, LANES) for h in range(s.halves)]
        own_columns[...] = dot(jnp.concatenate(held, axis=1), spread).astype(BF16)

    clip = clip_rows[...]
    clip_squared = clip * clip

    own, before, after = left_blocks[0], left_blocks[1 : s.n_rcv], left_blocks[s.n_rcv :]
    blocks = []
    for place in range(s.n_rcv):
        block = own[...]
        for at in range(s.n_rcv):
            if at > place:
                block = jnp.where(rcv == at, before[at - place - 1][...], block)
            elif at < place:
                block = jnp.where(rcv == at, after[place - at - 1][...], block)
        blocks.append(block.astype(F32))
    plain = jnp.concatenate(blocks, axis=1)
    lane = lax.broadcasted_iota(jnp.int32, (tile_rows, s.depth), 1)
    is_real = (lane // s.own) % 2 == 0
    swapped = jnp.where(
        is_real,
        pltpu.roll(plain, s.depth - s.own, 1),
        pltpu.roll(plain, s.own, 1),
    )
    sign = jnp.where(is_real, 1.0, -1.0)
    signed = plain * sign
    left[:tile_rows] = signed.astype(BF16)
    left[tile_rows : 2 * tile_rows] = swapped.astype(BF16)

    product = dot(left[: 2 * tile_rows], own_columns[...])
    real, imag = product[:tile_rows], product[tile_rows:]
    limiter = limited(real, imag, clip, clip_squared)
    real, imag = real * limiter, imag * limiter
    left[2 * tile_rows : 3 * tile_rows] = (signed - jnp.where(is_real, real, -imag)).astype(BF16)
    left[3 * tile_rows :] = (swapped - jnp.where(is_real, imag, real)).astype(BF16)

    for tile in range(s.slots // tile_slots):
        place = slice(tile * width, (tile + 1) * width)
        slots = range(tile * tile_slots, (tile + 1) * tile_slots)
        pieces = [right[:, slot].reshape(s.depth, LANES) for slot in slots]
        product = dot(left[...], jnp.concatenate(pieces, axis=1))
        base_real = recorded[0, :, place].astype(F32)
        base_imag = recorded[1, :, place].astype(F32)
        for which, out in enumerate((out_first, out_second)):
            first = 2 * which * tile_rows
            real = product[first : first + tile_rows]
            imag = product[first + tile_rows : first + 2 * tile_rows]
            limiter = limited(real, imag, clip, clip_squared)
            out[0, :, place] = (base_real - real * limiter).astype(BF16)
            out[1, :, place] = (base_imag - imag * limiter).astype(BF16)


def update(recorded, clip_level, left_blocks, filtered, s):
    tile_rows, tile_slots = 128, 2
    block = pl.BlockSpec((2, tile_rows, s.cols), lambda i: (0, i, 0))
    left_block = pl.BlockSpec((tile_rows, LANES), lambda i: (i, 0))
    places = s.n_src * s.n_rcv
    product_flops = 16 * s.rows * s.cols * PANEL
    return pl.pallas_call(
        functools.partial(update_kernel, s, tile_rows, tile_slots),
        grid=(s.rows // tile_rows,),
        in_specs=[block, pl.BlockSpec((tile_rows, 1), lambda i: (i, 0))]
        + [left_block] * len(left_blocks)
        + [pl.BlockSpec(memory_space=pl.ANY)] * places,
        out_specs=[block, block],
        out_shape=[jax.ShapeDtypeStruct(recorded.shape, BF16)] * 2,
        scratch_shapes=[
            pltpu.VMEM((places, s.slots + s.halves, 2 * s.own, LANES), BF16),
            pltpu.VMEM((s.depth, s.depth), BF16),
            pltpu.VMEM((4 * tile_rows, s.depth), BF16),
            pltpu.SemaphoreType.DMA((places,)),
        ],
        compiler_params=pltpu.CompilerParams(vmem_limit_bytes=VMEM_BYTES),
        cost_estimate=pl.CostEstimate(
            flops=product_flops, bytes_accessed=6 * 2 * s.rows * s.cols, transcendentals=0
        ),
        name="update",
    )(recorded, clip_level[:, None], *left_blocks, *filtered)


def rotate(block, ahead, count):
    pairs = [(at, (at + ahead) % count) for at in range(count)]
    return lax.ppermute(block, "rcv", pairs)


def exchange(blocks, count):
    return [blocks[0]] + [rotate(blocks[k], k, count) for k in range(1, count)]


def gather_line(block, count):
    up = [(at, at + 1) for at in range(count - 1)]
    down = [(at + 1, at) for at in range(count - 1)]
    before, after = [], []
    up_block = down_block = block
    for _ in range(count - 1):
        up_block = lax.ppermute(up_block, "rcv", up)
        down_block = lax.ppermute(down_block, "rcv", down)
        before.append(up_block)
        after.append(down_block)
    return [block] + before + after


def gather_cube(pieces, count):
    steps = [1 << bit for bit in range(1, count.bit_length() - 1)]
    half = len(pieces) // 2
    gathered = {}
    for order, part in ((steps, range(half)), (steps[::-1], range(half, len(pieces)))):
        for which in part:
            held = {0: pieces[which]}
            for step in order:
                pairs = [(at, at ^ step) for at in range(count)]
                held.update(
                    {d ^ step: lax.ppermute(p, "src", pairs) for d, p in sorted(held.items())}
                )
            pairs = [(at, at ^ 1) for at in range(count)]
            held.update({d ^ 1: lax.ppermute(p, "src", pairs) for d, p in sorted(held.items())})
            for d, p in held.items():
                gathered[d, which] = p
    return [gathered[d, which] for d in range(count) for which in range(len(pieces))]


def per_device(recorded, obliquity, clip_level):
    s = Sizes(recorded, lax.axis_size("src"), lax.axis_size("rcv"))
    if not s.fits():
        return plain_device(recorded, obliquity, clip_level)
    moved = exchange(pick_rows(recorded, s), s.n_rcv)
    left_blocks = gather_line(pick_columns(recorded, s), s.n_rcv)
    returned = exchange(filter_rows(moved, obliquity, s), s.n_rcv)
    filtered = gather_cube(returned, s.n_src)
    return update(recorded, clip_level, left_blocks, filtered, s)


def solution(mesh):
    return jax.shard_map(
        per_device,
        mesh=mesh,
        in_specs=(P(None, "src", "rcv"), P(), P("src")),
        out_specs=(P(None, "src", "rcv"), P(None, "src", "rcv")),
        check_vma=False,
    )
```

```python
import functools
import math

import jax
import jax.numpy as jnp
import numpy as np
from jax import lax
from jax.experimental import pallas as pl
from jax.experimental.pallas import tpu as pltpu
from jax.sharding import PartitionSpec as P

LANES = 128
PANEL = 256
PIECES = 1
ROW_BLOCK = 256
PICK_ROWS = 512
EARLY = 1
BF16 = jnp.bfloat16
F32 = jnp.float32
VMEM_BYTES = 56 * 2**20


class Sizes:
    def __init__(self, recorded, n_src, n_rcv):
        self.n_src, self.n_rcv = n_src, n_rcv
        self.rows, self.cols = recorded.shape[1], recorded.shape[2]
        self.order = self.cols * n_rcv
        self.spacing = self.order // PANEL
        self.group = PANEL // n_src
        self.own = self.group // n_rcv
        self.panel_cols = PANEL // n_rcv
        self.slots = self.cols // LANES
        self.points = self.order // LANES
        self.halves = LANES // self.spacing
        self.depth = 2 * PANEL

    def spans(self, extra=0):
        count = self.slots // PIECES
        return [(q * count, count + (extra if q == 0 else 0)) for q in range(PIECES)]

    def fits(self):
        return (
            self.points == LANES
            and self.n_src & (self.n_src - 1) == 0
            and self.n_src > 2
            and self.n_rcv % 2 == 0
            and self.group % self.n_rcv == 0
            and self.own % 8 == 0
            and self.panel_cols % self.group == 0
            and 2 * self.panel_cols == LANES
            and self.spacing % 16 == 0
            and self.slots % 16 == 0
            and self.halves * LANES == PANEL
            and self.rows % PICK_ROWS == 0
            and self.rows > PICK_ROWS
            and self.slots % (2 * PIECES) == 0
        )


def transform_tables(points, order, groups):
    index = np.arange(points)
    sorted_index = index.reshape(-1, groups).T.reshape(-1)
    angles = np.outer(sorted_index, index) % points * (2.0 * math.pi / points)
    cosine, sine = np.cos(angles), np.sin(angles)
    table = np.block([[cosine, sine], [-sine, cosine]]).astype(np.float32)
    high = table.astype(BF16)
    low = (table - high.astype(np.float32)).astype(BF16)
    turns = np.outer(sorted_index, np.arange(LANES)) % order * (2.0 * math.pi / order)
    factors = np.stack([np.cos(turns), np.sin(turns)]).astype(np.float32)
    return np.stack([high, low, high.T, low.T]), factors


def lane_parts(lane, s):
    group, rest = lane // (2 * s.group), lane % (2 * s.group)
    owner, rest = rest // (2 * s.own), rest % (2 * s.own)
    part, row = rest // s.own, rest % s.own
    return group * s.group + owner * s.own + row, part


def pick_rows_kernel(s, recorded, *refs):
    outs, (held, lines, sems) = refs[: s.n_rcv], refs[s.n_rcv :]
    me = lax.axis_index("rcv")

    def copy(index):
        ahead, row = index // s.own, index % s.own
        line = lax.rem(me + ahead, s.n_rcv) * s.own + row
        first = pl.multiple_of(line * s.spacing, 16)
        return pltpu.make_async_copy(
            recorded.at[:, pl.ds(first, 16), :], held.at[index], sems.at[index]
        )

    for index in range(s.group):
        copy(index).start()
    for index in range(s.group):
        copy(index).wait()
        for part in range(2):
            line = held[index, part].astype(F32)[0:1]
            for slot in range(s.slots):
                lines[slot : slot + 1, :] = line[:, slot * LANES : (slot + 1) * LANES]
            outs[index // s.own][index % s.own, part] = lines[...].astype(BF16)


def pick_rows(recorded, s):
    shape = (s.own, 2, s.slots, LANES)
    return pl.pallas_call(
        functools.partial(pick_rows_kernel, s),
        in_specs=[pl.BlockSpec(memory_space=pl.ANY)],
        out_shape=[jax.ShapeDtypeStruct(shape, BF16)] * s.n_rcv,
        scratch_shapes=[
            pltpu.VMEM((s.group, 2, 16, s.cols), BF16),
            pltpu.VMEM((s.slots, LANES), F32),
            pltpu.SemaphoreType.DMA((s.group,)),
        ],
        compiler_params=pltpu.CompilerParams(vmem_limit_bytes=VMEM_BYTES),
        name="pick_rows",
    )(recorded)


def pick_columns_kernel(s, chunk, recorded, *refs):
    out, select, total = refs[-3:]
    step = pl.program_id(0)
    receiver = step * chunk + lax.broadcasted_iota(jnp.int32, (chunk, LANES), 0)
    column, part = lane_parts(lax.broadcasted_iota(jnp.int32, (1, LANES), 1), s)
    for which in range(2):
        chosen = receiver == jnp.where(part == which, column * s.spacing, -1)
        select[which] = jnp.where(chosen, 1.0, 0.0).astype(BF16)
    picked = dot(recorded[0], select[0]) + dot(recorded[1], select[1])

    @pl.when(step == 0)
    def _():
        total[...] = picked

    @pl.when(step > 0)
    def _():
        total[...] += picked

    @pl.when(step == pl.num_programs(0) - 1)
    def _():
        out[...] = total[...].astype(BF16)


def pick_columns(recorded, first, count, chunk, behind, s):
    rows = count * PICK_ROWS
    return pl.pallas_call(
        functools.partial(pick_columns_kernel, s, chunk),
        grid=(s.cols // chunk,),
        in_specs=[
            pl.BlockSpec(
                (pl.Element(2), pl.Element(rows), pl.Element(chunk)),
                lambda i: (0, first * PICK_ROWS, i * chunk),
            ),
            pl.BlockSpec(memory_space=pl.ANY),
        ],
        out_specs=pl.BlockSpec((rows, LANES), lambda i: (0, 0)),
        out_shape=jax.ShapeDtypeStruct((rows, LANES), BF16),
        scratch_shapes=[pltpu.VMEM((2, chunk, LANES), BF16), pltpu.VMEM((rows, LANES), F32)],
        compiler_params=pltpu.CompilerParams(vmem_limit_bytes=VMEM_BYTES),
        cost_estimate=pl.CostEstimate(
            flops=8 * rows * s.cols * LANES,
            bytes_accessed=4 * rows * s.cols,
            transcendentals=0,
        ),
        name="pick_columns",
    )(recorded, behind)


def split(values):
    high = values.astype(BF16)
    return high, (values - high.astype(F32)).astype(BF16)


def dot(left, right):
    return jnp.dot(left, right, preferred_element_type=F32)


def filter_kernel(s, *refs):
    blocks, refs = refs[: s.n_rcv], refs[s.n_rcv :]
    tables, factors, obliquity = refs[:3]
    refs = refs[1:]
    spans = s.spans()
    outs = [refs[3 + q * s.n_rcv : 3 + (q + 1) * s.n_rcv] for q in range(len(spans))]
    values, joined, turned, sorted_rows, factor_rows, scale = refs[3 + len(spans) * s.n_rcv :]
    me = lax.axis_index("rcv")
    n = s.points
    lanes = [slice(r * LANES, (r + 1) * LANES) for r in range(s.own)]
    rows = [slice(r * n, (r + 1) * n) for r in range(s.own)]
    for behind in range(s.n_rcv):
        owner = lax.rem(me + s.n_rcv - behind, s.n_rcv)
        for part in range(2):
            place = pl.ds(pl.multiple_of(part * n + owner * s.slots, 16), s.slots)
            for r in range(s.own):
                values[place, lanes[r]] = blocks[behind][r, part]

    groups, m = obliquity.shape[0], s.points // obliquity.shape[0]
    for a in range(groups):
        for tile in range(m):
            line = slice(a * m + tile, a * m + tile + 1)
            factor_rows[line, :] = obliquity[a : a + 1, tile * LANES : (tile + 1) * LANES]
    turned_rows = jnp.transpose(factor_rows[...])
    for a in range(groups):
        for q in range(groups):
            block = turned_rows[q * m : (q + 1) * m, a * m : (a + 1) * m]
            scale[a * m : (a + 1) * m, q * m : (q + 1) * m] = block
            scale[a * m : (a + 1) * m, LANES + q * m : LANES + (q + 1) * m] = block

    cosine, sine = factors[0], factors[1]
    first = dot(tables[0], values[...]) + dot(tables[1], values[...])
    for r in range(s.own):
        real, imag = first[:n, lanes[r]], first[n:, lanes[r]]
        joined[rows[r], :LANES] = real * cosine + imag * sine
        joined[rows[r], LANES:] = imag * cosine - real * sine
    high, low = split(joined[...])
    spectrum = dot(high, tables[2]) + (dot(high, tables[3]) + dot(low, tables[2]))
    for r in range(s.own):
        joined[rows[r], :] = spectrum[rows[r]] * scale[...]
    high, low = split(joined[...])
    back = dot(high, tables[0]) + (dot(high, tables[1]) + dot(low, tables[0]))
    cosine, sine = cosine * (1.0 / s.order), sine * (1.0 / s.order)
    for r in range(s.own):
        real, imag = back[rows[r], :LANES], back[rows[r], LANES:]
        turned[:n, lanes[r]] = real * cosine - imag * sine
        turned[n:, lanes[r]] = real * sine + imag * cosine
    high, low = split(turned[...])
    result = dot(tables[2], high) + (dot(tables[3], high) + dot(tables[2], low))

    shape = (s.halves * s.own, s.own * LANES)
    wanted = lax.broadcasted_iota(jnp.int32, shape, 0)
    lane = lax.broadcasted_iota(jnp.int32, shape, 1)
    chosen = lane == (wanted % s.own) * LANES + (wanted // s.own) * s.spacing
    select = jnp.where(chosen, 1.0, 0.0).astype(BF16)
    rounded = result.astype(BF16)
    picked = [
        lax.dot_general(
            select,
            rounded[part * n : (part + 1) * n],
            (((1,), (1,)), ((), ())),
            preferred_element_type=F32,
        )
        for part in range(2)
    ]
    for half in range(s.halves):
        place = slice(half * s.own, (half + 1) * s.own)
        extra = jnp.concatenate([picked[0][place], picked[1][place]], axis=0).astype(BF16)
        for out in outs[0]:
            out[spans[0][1] + half] = extra

    height = 2 * s.own
    for part in range(2):
        for r in range(s.own):
            place = pl.ds(part * s.own + r, n, stride=height)
            sorted_rows[place, :] = result[part * n : (part + 1) * n, lanes[r]]
    for ahead in range(s.n_rcv):
        owner = lax.rem(me + ahead, s.n_rcv)
        for out, (start, count) in zip(outs, spans):
            first_row = pl.multiple_of((owner * s.slots + start) * height, 16)
            mine = sorted_rows[pl.ds(first_row, count * height), :]
            out[ahead][:count] = mine.reshape(count, height, LANES).astype(BF16)


def filter_rows(blocks, obliquity, behind, s):
    tables, factors = transform_tables(s.points, s.order, obliquity.shape[0])
    shapes = [(count, 2 * s.own, LANES) for _, count in s.spans(s.halves)]
    outs = pl.pallas_call(
        functools.partial(filter_kernel, s),
        in_specs=[pl.BlockSpec(memory_space=pltpu.VMEM)] * (s.n_rcv + 3)
        + [pl.BlockSpec(memory_space=pl.ANY)],
        out_shape=[jax.ShapeDtypeStruct(shape, BF16) for shape in shapes for _ in range(s.n_rcv)],
        scratch_shapes=[
            pltpu.VMEM((2 * s.points, s.own * LANES), BF16),
            pltpu.VMEM((s.own * s.points, 2 * LANES), F32),
            pltpu.VMEM((2 * s.points, s.own * LANES), F32),
            pltpu.VMEM((2 * s.own * s.points, LANES), F32),
            pltpu.VMEM((s.points, LANES), F32),
            pltpu.VMEM((s.points, 2 * LANES), F32),
        ],
        compiler_params=pltpu.CompilerParams(vmem_limit_bytes=VMEM_BYTES),
        name="filter_rows",
    )(*blocks, jnp.asarray(tables), jnp.asarray(factors), obliquity, behind)
    return [outs[q * s.n_rcv : (q + 1) * s.n_rcv] for q in range(len(shapes))]


TWO_PI = 2.0 * math.pi


def turn(real_part, imag_part, cosine, sine_part):
    return (real_part * cosine - imag_part * sine_part, real_part * sine_part + imag_part * cosine)


def twiddle(real_part, imag_part, column_index, group_index, orient, total_length):
    angles = (column_index * group_index % total_length).astype(jnp.float32) * (
        TWO_PI / total_length
    )
    return turn(real_part, imag_part, jnp.cos(angles), orient * jnp.sin(angles))


def long_table(length, orient):
    index_left = lax.broadcasted_iota(jnp.int32, (length, length), 0)
    index_right = lax.broadcasted_iota(jnp.int32, (length, length), 1)
    angles = (index_left * index_right % length).astype(jnp.float32) * (TWO_PI / length)
    cosine = jnp.cos(angles)
    sine_part = orient * jnp.sin(angles)
    upper = jnp.concatenate([cosine, sine_part], axis=1)
    lower = jnp.concatenate([-sine_part, cosine], axis=1)
    return jnp.concatenate([upper, lower], axis=0)


def long_transform(real_part, imag_part, orient):
    length = real_part.shape[-1]
    joined = jnp.concatenate([real_part, imag_part], axis=-1)
    result = jnp.dot(
        joined.reshape(-1, 2 * length),
        long_table(length, orient),
        precision=lax.Precision.HIGHEST,
        preferred_element_type=jnp.float32,
    )
    result = result.reshape(joined.shape)
    return (result[..., :length], result[..., length:])


def across_groups(real_part, imag_part, groups, orient):
    index_left = lax.broadcasted_iota(jnp.int32, (groups, groups), 0)
    index_right = lax.broadcasted_iota(jnp.int32, (groups, groups), 1)
    angles = (index_left * index_right % groups).astype(jnp.float32) * (TWO_PI / groups)
    cosine = jnp.cos(angles)
    sine_part = orient * jnp.sin(angles)
    highest = lax.Precision.HIGHEST
    new_real = jnp.einsum("mgc,gk->mkc", real_part, cosine, precision=highest) - jnp.einsum(
        "mgc,gk->mkc", imag_part, sine_part, precision=highest
    )
    new_imag = jnp.einsum("mgc,gk->mkc", real_part, sine_part, precision=highest) + jnp.einsum(
        "mgc,gk->mkc", imag_part, cosine, precision=highest
    )
    return (new_real, new_imag)


def plain_filter(whole_rows, obliquity, groups):
    row_total = whole_rows.shape[1]
    group_cols = whole_rows.shape[2] // groups
    total_length = groups * group_cols
    values = whole_rows.astype(jnp.float32).reshape(2, row_total, groups, group_cols)
    real_part, imag_part = across_groups(values[0], values[1], groups, -1.0)
    column_index = lax.broadcasted_iota(jnp.int32, (1, 1, group_cols), 2)
    group_index = lax.broadcasted_iota(jnp.int32, (1, groups, 1), 1)
    real_part, imag_part = twiddle(
        real_part, imag_part, column_index, group_index, -1.0, total_length
    )
    real_part, imag_part = long_transform(real_part, imag_part, -1.0)
    real_part = real_part * obliquity[None]
    imag_part = imag_part * obliquity[None]
    real_part, imag_part = long_transform(real_part, imag_part, 1.0)
    real_part, imag_part = twiddle(
        real_part, imag_part, column_index, group_index, 1.0, total_length
    )
    real_part, imag_part = across_groups(real_part, imag_part, groups, 1.0)
    inverse_scale = 1.0 / total_length
    returned = jnp.stack([real_part * inverse_scale, imag_part * inverse_scale])
    return returned.reshape(2, row_total, total_length).astype(jnp.bfloat16)


def through_rows(panel_rows, obliquity):
    moved_rows = lax.all_to_all(panel_rows, "rcv", split_axis=1, concat_axis=2, tiled=True)
    returned = plain_filter(moved_rows, obliquity, lax.axis_size("rcv"))
    return lax.all_to_all(returned, "rcv", split_axis=2, concat_axis=1, tiled=True)


def complex_product(left_rows, right_rows):
    left_joined = jnp.concatenate([left_rows[0], left_rows[1]], axis=0)
    upper = jnp.concatenate([right_rows[0], right_rows[1]], axis=1)
    lower = jnp.concatenate([-right_rows[1], right_rows[0]], axis=1)
    right_joined = jnp.concatenate([upper, lower], axis=0)
    return lax.dot_general(
        left_joined, right_joined, (((0,), (0,)), ((), ())), preferred_element_type=jnp.float32
    )


def plain_device(recorded, obliquity, clip_level):
    spacing = recorded.shape[2] * lax.axis_size("rcv") // PANEL
    row_total = recorded.shape[1]
    col_total = recorded.shape[2]
    panel_rows = recorded.reshape(2, row_total // spacing, spacing, col_total)[:, :, 0, :]
    filtered = through_rows(panel_rows, obliquity)
    clip_rows = clip_level[:, None]
    estimate = recorded
    passes = []
    for update_index in range(2):
        columns = estimate.reshape(2, row_total, col_total // spacing, spacing)[:, :, :, 0]
        left_local = jnp.swapaxes(columns, 1, 2)
        left_panel = lax.all_gather(left_local, "rcv", axis=1, tiled=True)

        def accumulate(running, panel_piece, first_row, left_all=left_panel):
            return complex_product(left_all, panel_piece)

        zeros_init = jnp.zeros((row_total, 2 * col_total), jnp.float32)
        product_sum = accumulate(
            zeros_init, lax.all_gather(filtered, "src", axis=1, tiled=True), jnp.int32(0)
        )
        pred_real = product_sum[:, :col_total]
        pred_imag = product_sum[:, col_total:]
        limiter = lax.rsqrt(
            1.0 + (pred_real * pred_real + pred_imag * pred_imag) / (clip_rows * clip_rows)
        )
        estimate = (
            recorded.astype(jnp.float32) - jnp.stack([pred_real * limiter, pred_imag * limiter])
        ).astype(jnp.bfloat16)
        passes.append(estimate)
    return (passes[0], passes[1])


def limited(real, imag, clip, clip_squared):
    return clip * lax.rsqrt(clip_squared + (real * real + imag * imag))


def left_rows(s, left_held, rows, clip, own_columns, left):
    rcv = lax.axis_index("rcv")
    count = rows.size
    blocks = []
    for place in range(s.n_rcv):
        block = left_held[0, rows, :]
        for at in range(s.n_rcv):
            if at != place:
                source = left_held[route(at, place, s.n_rcv), rows, :]
                block = jnp.where(rcv == at, source, block)
        blocks.append(block.astype(F32))
    plain = jnp.concatenate(blocks, axis=1)
    lane = lax.broadcasted_iota(jnp.int32, (1, s.depth), 1)
    is_real = (lane // s.own) % 2 == 0
    swapped = jnp.where(
        is_real,
        pltpu.roll(plain, s.depth - s.own, 1),
        pltpu.roll(plain, s.own, 1),
    )
    signed = jnp.where(is_real, plain, -plain)
    left[:count] = signed.astype(BF16)
    left[count : 2 * count] = swapped.astype(BF16)

    product = dot(left[: 2 * count], own_columns[...])
    real, imag = product[:count], product[count:]
    limiter = limited(real, imag, clip, clip * clip)
    real, imag = real * limiter, imag * limiter
    left[2 * count : 3 * count] = (signed - jnp.where(is_real, real, -imag)).astype(BF16)
    left[3 * count :] = (swapped - jnp.where(is_real, imag, real)).astype(BF16)


def update_kernel(s, tile_rows, tile_slots, *refs):
    recorded, clip_rows = refs[:2]
    split_at = len(refs) - 9 - 4
    left_blocks, filtered, refs = refs[2:split_at], refs[split_at:-9], refs[-9:]
    out_first, out_second, right, own_columns, even, odd, sems, left_sems, left_held = refs
    src, rcv = lax.axis_index("src"), lax.axis_index("rcv")
    width = tile_slots * LANES
    step, steps = pl.program_id(0), pl.num_programs(0)

    def fill(which, left):
        rows = pl.ds(pl.multiple_of(which * tile_rows, tile_rows), tile_rows)
        left_rows(s, left_held, rows, clip_rows[rows, :], own_columns, left)

    @pl.when(step == 0)
    def _():
        copies = []
        for mask in range(s.n_src):
            odd_mask, (half, at) = mask % 2, divmod(mask // 2, s.n_src // 4)
            for behind in range(s.n_rcv):
                owner = lax.rem(rcv + s.n_rcv - behind, s.n_rcv)
                place = (src ^ mask) * s.n_rcv + owner
                block = filtered[2 * odd_mask + half].at[at, behind]
                copies.append(
                    pltpu.make_async_copy(block, right.at[place], sems.at[len(copies)])
                )
        for index, block in enumerate(left_blocks):
            copies.append(
                pltpu.make_async_copy(block, left_held.at[index], left_sems.at[index])
            )
        for copy in copies:
            copy.start()
        for copy in copies:
            copy.wait()
        row = lax.broadcasted_iota(jnp.int32, (PANEL, s.depth), 0)
        lane = lax.broadcasted_iota(jnp.int32, (1, s.depth), 1)
        column, _part = lane_parts(lane % LANES, s)
        column = column + (lane // LANES) * s.panel_cols
        chosen = row == (column % s.halves) * LANES + column // s.halves
        spread = jnp.where(chosen, 1.0, 0.0).astype(BF16)
        held = [right[:, s.slots + h].reshape(s.depth, LANES) for h in range(s.halves)]
        own_columns[...] = dot(jnp.concatenate(held, axis=1), spread).astype(BF16)
        fill(0, even)

    def products(left, offset):
        rows = slice(offset, offset + tile_rows)
        clip = clip_rows[pl.ds(pl.multiple_of(step * 2 * tile_rows + offset, tile_rows), tile_rows), :]
        clip_squared = clip * clip
        for tile in range(s.slots // tile_slots):
            place = slice(tile * width, (tile + 1) * width)
            spots = range(tile * tile_slots, (tile + 1) * tile_slots)
            pieces = [right[:, spot].reshape(s.depth, LANES) for spot in spots]
            joined = jnp.concatenate(pieces, axis=1)
            base_real = recorded[0, rows, place].astype(F32)
            base_imag = recorded[1, rows, place].astype(F32)
            for which, out in enumerate((out_first, out_second)):
                first = 2 * which * tile_rows
                product = dot(left[first : first + 2 * tile_rows], joined)
                real, imag = product[:tile_rows], product[tile_rows:]
                limiter = limited(real, imag, clip, clip_squared)
                out[0, rows, place] = (base_real - real * limiter).astype(BF16)
                out[1, rows, place] = (base_imag - imag * limiter).astype(BF16)

    fill(2 * step + 1, odd)
    products(even, 0)
    fill(jnp.minimum(2 * step + 2, 2 * steps - 1), even)
    products(odd, tile_rows)


def update(recorded, clip_level, left_blocks, filtered, s):
    tile_rows, tile_slots = ROW_BLOCK // 2, 2
    places = s.n_src * s.n_rcv
    anywhere = pl.BlockSpec(memory_space=pl.ANY)
    block = pl.BlockSpec((2, 2 * tile_rows, s.cols), lambda i: (0, i, 0))
    return pl.pallas_call(
        functools.partial(update_kernel, s, tile_rows, tile_slots),
        grid=(s.rows // (2 * tile_rows),),
        in_specs=[block, pl.BlockSpec(memory_space=pltpu.VMEM)]
        + [anywhere] * (len(left_blocks) + len(filtered)),
        out_specs=[block, block],
        out_shape=[jax.ShapeDtypeStruct(recorded.shape, BF16)] * 2,
        scratch_shapes=[
            pltpu.VMEM((places, s.slots + s.halves, 2 * s.own, LANES), BF16),
            pltpu.VMEM((s.depth, s.depth), BF16),
            pltpu.VMEM((4 * tile_rows, s.depth), BF16),
            pltpu.VMEM((4 * tile_rows, s.depth), BF16),
            pltpu.SemaphoreType.DMA((places,)),
            pltpu.SemaphoreType.DMA((len(left_blocks),)),
            pltpu.VMEM((len(left_blocks), s.rows, LANES), BF16),
        ],
        compiler_params=pltpu.CompilerParams(vmem_limit_bytes=VMEM_BYTES),
        cost_estimate=pl.CostEstimate(
            flops=32 * s.rows * s.cols * PANEL,
            bytes_accessed=12 * s.rows * s.cols,
            transcendentals=0,
        ),
        name="update",
    )(recorded, clip_level[:, None], *left_blocks, *filtered)


def rotate(block, ahead, count):
    pairs = [(at, (at + ahead) % count) for at in range(count)]
    return lax.ppermute(block, "rcv", pairs)


def exchange(blocks, count):
    return [blocks[0]] + [rotate(blocks[k], k, count) for k in range(1, count)]


def route(at, place, count):
    if count != 4:
        return (at - place) % count
    return {0: 0, 1: 1, 2: 2, 3: 4}[at ^ place] if at ^ place != 3 or abs(at - place) == 3 else 3


def gather_both(block, pieces, s):
    def swap(held, axis, count, step):
        return lax.ppermute(held, axis, [(at, at ^ step) for at in range(count)])

    line = s.n_rcv == 4
    if line:
        far, outer = swap(block, "rcv", 4, 2), swap(block, "rcv", 4, 1)
        left = (far, outer)
    else:
        left = tuple(exchange([block] * s.n_rcv, s.n_rcv)[1:])
    chips = {step: swap(pieces, "src", s.n_src, step) for step in range(2, s.n_src, 2)}
    block, left, chips, pieces = lax.optimization_barrier((block, left, chips, pieces))
    chips[0] = pieces
    if line:
        far, outer = left
        ends = lax.ppermute(far, "rcv", [(1, 0), (2, 3)])
        middle = lax.ppermute(block, "rcv", [(1, 2), (2, 1)])
        left = (outer, far, middle, ends)
    count = s.n_src // 2
    halves = [range(0, count // 2), range(count // 2, count)]
    same = [jnp.stack([chips[2 * at] for at in half]) for half in halves]
    other = [swap(half, "src", s.n_src, 1) for half in same]
    return (block,) + left, same + other


def per_device(recorded, obliquity, clip_level):
    s = Sizes(recorded, lax.axis_size("src"), lax.axis_size("rcv"))
    if not s.fits():
        return plain_device(recorded, obliquity, clip_level)
    blocks = s.rows // PICK_ROWS
    picked_rows = pick_rows(recorded, s)
    moved = exchange(picked_rows, s.n_rcv)
    early = pick_columns(recorded, 0, EARLY, s.cols // 4, picked_rows[0], s)
    rows = filter_rows(moved, obliquity, early, s)[0]
    returned = exchange(rows, s.n_rcv)
    late = pick_columns(recorded, EARLY, blocks - EARLY, s.cols // 8, rows[0], s)
    pieces, columns = lax.optimization_barrier(
        (jnp.stack(returned), jnp.concatenate([early, late]))
    )
    left_blocks, filtered = gather_both(columns, pieces, s)
    return update(recorded, clip_level, left_blocks, filtered, s)


def solution(mesh):
    return jax.shard_map(
        per_device,
        mesh=mesh,
        in_specs=(P(None, "src", "rcv"), P(), P("src")),
        out_specs=(P(None, "src", "rcv"), P(None, "src", "rcv")),
        check_vma=False,
    )
```

```python
import functools
import math

import jax
import jax.numpy as jnp
import numpy as np
from jax import lax
from jax.experimental import pallas as pl
from jax.experimental.pallas import tpu as pltpu
from jax.sharding import PartitionSpec as P

LANES = 128
PANEL = 256
PIECES = 1
ROW_BLOCK = 256
PICK_ROWS = 512
EARLY = 1
BF16 = jnp.bfloat16
F32 = jnp.float32
VMEM_BYTES = 56 * 2**20


class Sizes:
    def __init__(self, recorded, n_src, n_rcv):
        self.n_src, self.n_rcv = n_src, n_rcv
        self.rows, self.cols = recorded.shape[1], recorded.shape[2]
        self.order = self.cols * n_rcv
        self.spacing = self.order // PANEL
        self.group = PANEL // n_src
        self.own = self.group // n_rcv
        self.panel_cols = PANEL // n_rcv
        self.slots = self.cols // LANES
        self.points = self.order // LANES
        self.halves = LANES // self.spacing
        self.depth = 2 * PANEL

    def spans(self, extra=0):
        count = self.slots // PIECES
        return [(q * count, count + (extra if q == 0 else 0)) for q in range(PIECES)]

    def fits(self):
        return (
            self.points == LANES
            and self.n_src & (self.n_src - 1) == 0
            and self.n_src > 2
            and self.n_rcv % 2 == 0
            and self.group % self.n_rcv == 0
            and self.own % 8 == 0
            and self.panel_cols % self.group == 0
            and 2 * self.panel_cols == LANES
            and self.spacing % 16 == 0
            and self.slots % 16 == 0
            and self.halves * LANES == PANEL
            and self.rows % PICK_ROWS == 0
            and self.rows > PICK_ROWS
            and self.slots % (2 * PIECES) == 0
        )


def transform_tables(points, order, groups):
    index = np.arange(points)
    sorted_index = index.reshape(-1, groups).T.reshape(-1)
    angles = np.outer(sorted_index, index) % points * (2.0 * math.pi / points)
    cosine, sine = np.cos(angles), np.sin(angles)
    table = np.block([[cosine, sine], [-sine, cosine]]).astype(np.float32)
    high = table.astype(BF16)
    low = (table - high.astype(np.float32)).astype(BF16)
    turns = np.outer(sorted_index, np.arange(LANES)) % order * (2.0 * math.pi / order)
    factors = np.stack([np.cos(turns), np.sin(turns)]).astype(np.float32)
    return np.stack([high, low, high.T, low.T]), factors


def lane_parts(lane, s):
    group, rest = lane // (2 * s.group), lane % (2 * s.group)
    owner, rest = rest // (2 * s.own), rest % (2 * s.own)
    part, row = rest // s.own, rest % s.own
    return group * s.group + owner * s.own + row, part


def pick_rows_kernel(s, recorded, *refs):
    outs, (held, lines, sems) = refs[: s.n_rcv], refs[s.n_rcv :]
    me = lax.axis_index("rcv")

    def copy(index):
        ahead, row = index // s.own, index % s.own
        line = lax.rem(me + ahead, s.n_rcv) * s.own + row
        first = pl.multiple_of(line * s.spacing, 16)
        return pltpu.make_async_copy(
            recorded.at[:, pl.ds(first, 16), :], held.at[index], sems.at[index]
        )

    for index in range(s.group):
        copy(index).start()
    for index in range(s.group):
        copy(index).wait()
        for part in range(2):
            line = held[index, part].astype(F32)[0:1]
            for slot in range(s.slots):
                lines[slot : slot + 1, :] = line[:, slot * LANES : (slot + 1) * LANES]
            outs[index // s.own][index % s.own, part] = lines[...].astype(BF16)


def pick_rows(recorded, s):
    shape = (s.own, 2, s.slots, LANES)
    return pl.pallas_call(
        functools.partial(pick_rows_kernel, s),
        in_specs=[pl.BlockSpec(memory_space=pl.ANY)],
        out_shape=[jax.ShapeDtypeStruct(shape, BF16)] * s.n_rcv,
        scratch_shapes=[
            pltpu.VMEM((s.group, 2, 16, s.cols), BF16),
            pltpu.VMEM((s.slots, LANES), F32),
            pltpu.SemaphoreType.DMA((s.group,)),
        ],
        compiler_params=pltpu.CompilerParams(vmem_limit_bytes=VMEM_BYTES),
        name="pick_rows",
    )(recorded)


def pick_columns_kernel(s, chunk, recorded, *refs):
    out, select, total = refs[-3:]
    step = pl.program_id(0)
    receiver = step * chunk + lax.broadcasted_iota(jnp.int32, (chunk, LANES), 0)
    column, part = lane_parts(lax.broadcasted_iota(jnp.int32, (1, LANES), 1), s)
    for which in range(2):
        chosen = receiver == jnp.where(part == which, column * s.spacing, -1)
        select[which] = jnp.where(chosen, 1.0, 0.0).astype(BF16)
    picked = dot(recorded[0], select[0]) + dot(recorded[1], select[1])

    @pl.when(step == 0)
    def _():
        total[...] = picked

    @pl.when(step > 0)
    def _():
        total[...] += picked

    @pl.when(step == pl.num_programs(0) - 1)
    def _():
        out[...] = total[...].astype(BF16)


def pick_columns(recorded, first, count, chunk, behind, s):
    rows = count * PICK_ROWS
    return pl.pallas_call(
        functools.partial(pick_columns_kernel, s, chunk),
        grid=(s.cols // chunk,),
        in_specs=[
            pl.BlockSpec(
                (pl.Element(2), pl.Element(rows), pl.Element(chunk)),
                lambda i: (0, first * PICK_ROWS, i * chunk),
            ),
            pl.BlockSpec(memory_space=pl.ANY),
        ],
        out_specs=pl.BlockSpec((rows, LANES), lambda i: (0, 0)),
        out_shape=jax.ShapeDtypeStruct((rows, LANES), BF16),
        scratch_shapes=[pltpu.VMEM((2, chunk, LANES), BF16), pltpu.VMEM((rows, LANES), F32)],
        compiler_params=pltpu.CompilerParams(vmem_limit_bytes=VMEM_BYTES),
        cost_estimate=pl.CostEstimate(
            flops=8 * rows * s.cols * LANES,
            bytes_accessed=4 * rows * s.cols,
            transcendentals=0,
        ),
        name="pick_columns",
    )(recorded, behind)


def split(values):
    high = values.astype(BF16)
    return high, (values - high.astype(F32)).astype(BF16)


def dot(left, right):
    return jnp.dot(left, right, preferred_element_type=F32)


def filter_kernel(s, *refs):
    blocks, refs = refs[: s.n_rcv], refs[s.n_rcv :]
    tables, factors, obliquity = refs[:3]
    refs = refs[1:]
    spans = s.spans()
    outs = [refs[3 + q * s.n_rcv : 3 + (q + 1) * s.n_rcv] for q in range(len(spans))]
    values, joined, turned, sorted_rows, factor_rows, scale = refs[3 + len(spans) * s.n_rcv :]
    me = lax.axis_index("rcv")
    n = s.points
    lanes = [slice(r * LANES, (r + 1) * LANES) for r in range(s.own)]
    rows = [slice(r * n, (r + 1) * n) for r in range(s.own)]
    for behind in range(s.n_rcv):
        owner = lax.rem(me + s.n_rcv - behind, s.n_rcv)
        for part in range(2):
            place = pl.ds(pl.multiple_of(part * n + owner * s.slots, 16), s.slots)
            for r in range(s.own):
                values[place, lanes[r]] = blocks[behind][r, part]

    groups, m = obliquity.shape[0], s.points // obliquity.shape[0]
    for a in range(groups):
        for tile in range(m):
            line = slice(a * m + tile, a * m + tile + 1)
            factor_rows[line, :] = obliquity[a : a + 1, tile * LANES : (tile + 1) * LANES]
    turned_rows = jnp.transpose(factor_rows[...])
    for a in range(groups):
        for q in range(groups):
            block = turned_rows[q * m : (q + 1) * m, a * m : (a + 1) * m]
            scale[a * m : (a + 1) * m, q * m : (q + 1) * m] = block
            scale[a * m : (a + 1) * m, LANES + q * m : LANES + (q + 1) * m] = block

    cosine, sine = factors[0], factors[1]
    first = dot(tables[0], values[...]) + dot(tables[1], values[...])
    for r in range(s.own):
        real, imag = first[:n, lanes[r]], first[n:, lanes[r]]
        joined[rows[r], :LANES] = real * cosine + imag * sine
        joined[rows[r], LANES:] = imag * cosine - real * sine
    high, low = split(joined[...])
    spectrum = dot(high, tables[2]) + (dot(high, tables[3]) + dot(low, tables[2]))
    for r in range(s.own):
        joined[rows[r], :] = spectrum[rows[r]] * scale[...]
    high, low = split(joined[...])
    back = dot(high, tables[0]) + (dot(high, tables[1]) + dot(low, tables[0]))
    cosine, sine = cosine * (1.0 / s.order), sine * (1.0 / s.order)
    for r in range(s.own):
        real, imag = back[rows[r], :LANES], back[rows[r], LANES:]
        turned[:n, lanes[r]] = real * cosine - imag * sine
        turned[n:, lanes[r]] = real * sine + imag * cosine
    high, low = split(turned[...])
    result = dot(tables[2], high) + (dot(tables[3], high) + dot(tables[2], low))

    shape = (s.halves * s.own, s.own * LANES)
    wanted = lax.broadcasted_iota(jnp.int32, shape, 0)
    lane = lax.broadcasted_iota(jnp.int32, shape, 1)
    chosen = lane == (wanted % s.own) * LANES + (wanted // s.own) * s.spacing
    select = jnp.where(chosen, 1.0, 0.0).astype(BF16)
    rounded = result.astype(BF16)
    picked = [
        lax.dot_general(
            select,
            rounded[part * n : (part + 1) * n],
            (((1,), (1,)), ((), ())),
            preferred_element_type=F32,
        )
        for part in range(2)
    ]
    for half in range(s.halves):
        place = slice(half * s.own, (half + 1) * s.own)
        extra = jnp.concatenate([picked[0][place], picked[1][place]], axis=0).astype(BF16)
        for out in outs[0]:
            out[spans[0][1] + half] = extra

    height = 2 * s.own
    for part in range(2):
        for r in range(s.own):
            place = pl.ds(part * s.own + r, n, stride=height)
            sorted_rows[place, :] = result[part * n : (part + 1) * n, lanes[r]]
    for ahead in range(s.n_rcv):
        owner = lax.rem(me + ahead, s.n_rcv)
        for out, (start, count) in zip(outs, spans):
            first_row = pl.multiple_of((owner * s.slots + start) * height, 16)
            mine = sorted_rows[pl.ds(first_row, count * height), :]
            out[ahead][:count] = mine.reshape(count, height, LANES).astype(BF16)


def filter_rows(blocks, obliquity, behind, s):
    tables, factors = transform_tables(s.points, s.order, obliquity.shape[0])
    shapes = [(count, 2 * s.own, LANES) for _, count in s.spans(s.halves)]
    outs = pl.pallas_call(
        functools.partial(filter_kernel, s),
        in_specs=[pl.BlockSpec(memory_space=pltpu.VMEM)] * (s.n_rcv + 3)
        + [pl.BlockSpec(memory_space=pl.ANY)],
        out_shape=[jax.ShapeDtypeStruct(shape, BF16) for shape in shapes for _ in range(s.n_rcv)],
        scratch_shapes=[
            pltpu.VMEM((2 * s.points, s.own * LANES), BF16),
            pltpu.VMEM((s.own * s.points, 2 * LANES), F32),
            pltpu.VMEM((2 * s.points, s.own * LANES), F32),
            pltpu.VMEM((2 * s.own * s.points, LANES), F32),
            pltpu.VMEM((s.points, LANES), F32),
            pltpu.VMEM((s.points, 2 * LANES), F32),
        ],
        compiler_params=pltpu.CompilerParams(vmem_limit_bytes=VMEM_BYTES),
        name="filter_rows",
    )(*blocks, jnp.asarray(tables), jnp.asarray(factors), obliquity, behind)
    return [outs[q * s.n_rcv : (q + 1) * s.n_rcv] for q in range(len(shapes))]


TWO_PI = 2.0 * math.pi


def turn(real_part, imag_part, cosine, sine_part):
    return (real_part * cosine - imag_part * sine_part, real_part * sine_part + imag_part * cosine)


def twiddle(real_part, imag_part, column_index, group_index, orient, total_length):
    angles = (column_index * group_index % total_length).astype(jnp.float32) * (
        TWO_PI / total_length
    )
    return turn(real_part, imag_part, jnp.cos(angles), orient * jnp.sin(angles))


def long_table(length, orient):
    index_left = lax.broadcasted_iota(jnp.int32, (length, length), 0)
    index_right = lax.broadcasted_iota(jnp.int32, (length, length), 1)
    angles = (index_left * index_right % length).astype(jnp.float32) * (TWO_PI / length)
    cosine = jnp.cos(angles)
    sine_part = orient * jnp.sin(angles)
    upper = jnp.concatenate([cosine, sine_part], axis=1)
    lower = jnp.concatenate([-sine_part, cosine], axis=1)
    return jnp.concatenate([upper, lower], axis=0)


def long_transform(real_part, imag_part, orient):
    length = real_part.shape[-1]
    joined = jnp.concatenate([real_part, imag_part], axis=-1)
    result = jnp.dot(
        joined.reshape(-1, 2 * length),
        long_table(length, orient),
        precision=lax.Precision.HIGHEST,
        preferred_element_type=jnp.float32,
    )
    result = result.reshape(joined.shape)
    return (result[..., :length], result[..., length:])


def across_groups(real_part, imag_part, groups, orient):
    index_left = lax.broadcasted_iota(jnp.int32, (groups, groups), 0)
    index_right = lax.broadcasted_iota(jnp.int32, (groups, groups), 1)
    angles = (index_left * index_right % groups).astype(jnp.float32) * (TWO_PI / groups)
    cosine = jnp.cos(angles)
    sine_part = orient * jnp.sin(angles)
    highest = lax.Precision.HIGHEST
    new_real = jnp.einsum("mgc,gk->mkc", real_part, cosine, precision=highest) - jnp.einsum(
        "mgc,gk->mkc", imag_part, sine_part, precision=highest
    )
    new_imag = jnp.einsum("mgc,gk->mkc", real_part, sine_part, precision=highest) + jnp.einsum(
        "mgc,gk->mkc", imag_part, cosine, precision=highest
    )
    return (new_real, new_imag)


def plain_filter(whole_rows, obliquity, groups):
    row_total = whole_rows.shape[1]
    group_cols = whole_rows.shape[2] // groups
    total_length = groups * group_cols
    values = whole_rows.astype(jnp.float32).reshape(2, row_total, groups, group_cols)
    real_part, imag_part = across_groups(values[0], values[1], groups, -1.0)
    column_index = lax.broadcasted_iota(jnp.int32, (1, 1, group_cols), 2)
    group_index = lax.broadcasted_iota(jnp.int32, (1, groups, 1), 1)
    real_part, imag_part = twiddle(
        real_part, imag_part, column_index, group_index, -1.0, total_length
    )
    real_part, imag_part = long_transform(real_part, imag_part, -1.0)
    real_part = real_part * obliquity[None]
    imag_part = imag_part * obliquity[None]
    real_part, imag_part = long_transform(real_part, imag_part, 1.0)
    real_part, imag_part = twiddle(
        real_part, imag_part, column_index, group_index, 1.0, total_length
    )
    real_part, imag_part = across_groups(real_part, imag_part, groups, 1.0)
    inverse_scale = 1.0 / total_length
    returned = jnp.stack([real_part * inverse_scale, imag_part * inverse_scale])
    return returned.reshape(2, row_total, total_length).astype(jnp.bfloat16)


def through_rows(panel_rows, obliquity):
    moved_rows = lax.all_to_all(panel_rows, "rcv", split_axis=1, concat_axis=2, tiled=True)
    returned = plain_filter(moved_rows, obliquity, lax.axis_size("rcv"))
    return lax.all_to_all(returned, "rcv", split_axis=2, concat_axis=1, tiled=True)


def complex_product(left_rows, right_rows):
    left_joined = jnp.concatenate([left_rows[0], left_rows[1]], axis=0)
    upper = jnp.concatenate([right_rows[0], right_rows[1]], axis=1)
    lower = jnp.concatenate([-right_rows[1], right_rows[0]], axis=1)
    right_joined = jnp.concatenate([upper, lower], axis=0)
    return lax.dot_general(
        left_joined, right_joined, (((0,), (0,)), ((), ())), preferred_element_type=jnp.float32
    )


def plain_device(recorded, obliquity, clip_level):
    spacing = recorded.shape[2] * lax.axis_size("rcv") // PANEL
    row_total = recorded.shape[1]
    col_total = recorded.shape[2]
    panel_rows = recorded.reshape(2, row_total // spacing, spacing, col_total)[:, :, 0, :]
    filtered = through_rows(panel_rows, obliquity)
    clip_rows = clip_level[:, None]
    estimate = recorded
    passes = []
    for update_index in range(2):
        columns = estimate.reshape(2, row_total, col_total // spacing, spacing)[:, :, :, 0]
        left_local = jnp.swapaxes(columns, 1, 2)
        left_panel = lax.all_gather(left_local, "rcv", axis=1, tiled=True)

        def accumulate(running, panel_piece, first_row, left_all=left_panel):
            return complex_product(left_all, panel_piece)

        zeros_init = jnp.zeros((row_total, 2 * col_total), jnp.float32)
        product_sum = accumulate(
            zeros_init, lax.all_gather(filtered, "src", axis=1, tiled=True), jnp.int32(0)
        )
        pred_real = product_sum[:, :col_total]
        pred_imag = product_sum[:, col_total:]
        limiter = lax.rsqrt(
            1.0 + (pred_real * pred_real + pred_imag * pred_imag) / (clip_rows * clip_rows)
        )
        estimate = (
            recorded.astype(jnp.float32) - jnp.stack([pred_real * limiter, pred_imag * limiter])
        ).astype(jnp.bfloat16)
        passes.append(estimate)
    return (passes[0], passes[1])


def limited(real, imag, clip, clip_squared):
    return clip * lax.rsqrt(clip_squared + (real * real + imag * imag))


def left_rows(s, left_held, rows, clip, own_columns, left):
    rcv = lax.axis_index("rcv")
    count = rows.size
    blocks = []
    for place in range(s.n_rcv):
        block = left_held[0, rows, :]
        for at in range(s.n_rcv):
            if at != place:
                source = left_held[route(at, place, s.n_rcv), rows, :]
                block = jnp.where(rcv == at, source, block)
        blocks.append(block.astype(F32))
    plain = jnp.concatenate(blocks, axis=1)
    lane = lax.broadcasted_iota(jnp.int32, (1, s.depth), 1)
    is_real = (lane // s.own) % 2 == 0
    swapped = jnp.where(
        is_real,
        pltpu.roll(plain, s.depth - s.own, 1),
        pltpu.roll(plain, s.own, 1),
    )
    signed = jnp.where(is_real, plain, -plain)
    left[:count] = signed.astype(BF16)
    left[count : 2 * count] = swapped.astype(BF16)

    product = dot(left[: 2 * count], own_columns[...])
    real, imag = product[:count], product[count:]
    limiter = limited(real, imag, clip, clip * clip)
    real, imag = real * limiter, imag * limiter
    left[2 * count : 3 * count] = (signed - jnp.where(is_real, real, -imag)).astype(BF16)
    left[3 * count :] = (swapped - jnp.where(is_real, imag, real)).astype(BF16)


def update_kernel(s, tile_rows, tile_slots, *refs):
    recorded, clip_rows = refs[:2]
    split_at = len(refs) - 9 - 4
    left_blocks, filtered, refs = refs[2:split_at], refs[split_at:-9], refs[-9:]
    out_first, out_second, right, own_columns, even, odd, sems, left_sems, left_held = refs
    src, rcv = lax.axis_index("src"), lax.axis_index("rcv")
    width = tile_slots * LANES
    step, steps = pl.program_id(0), pl.num_programs(0)

    def fill(which, left):
        rows = pl.ds(pl.multiple_of(which * tile_rows, tile_rows), tile_rows)
        left_rows(s, left_held, rows, clip_rows[rows, :], own_columns, left)

    @pl.when(step == 0)
    def _():
        copies = []
        for mask in range(s.n_src):
            odd_mask, (half, at) = mask % 2, divmod(mask // 2, s.n_src // 4)
            for behind in range(s.n_rcv):
                owner = lax.rem(rcv + s.n_rcv - behind, s.n_rcv)
                place = (src ^ mask) * s.n_rcv + owner
                block = filtered[2 * odd_mask + half].at[at, behind]
                copies.append(
                    pltpu.make_async_copy(block, right.at[place], sems.at[len(copies)])
                )
        for index, block in enumerate(left_blocks):
            copies.append(
                pltpu.make_async_copy(block, left_held.at[index], left_sems.at[index])
            )
        for copy in copies:
            copy.start()
        for copy in copies:
            copy.wait()
        row = lax.broadcasted_iota(jnp.int32, (PANEL, s.depth), 0)
        lane = lax.broadcasted_iota(jnp.int32, (1, s.depth), 1)
        column, _part = lane_parts(lane % LANES, s)
        column = column + (lane // LANES) * s.panel_cols
        chosen = row == (column % s.halves) * LANES + column // s.halves
        spread = jnp.where(chosen, 1.0, 0.0).astype(BF16)
        held = [right[:, s.slots + h].reshape(s.depth, LANES) for h in range(s.halves)]
        own_columns[...] = dot(jnp.concatenate(held, axis=1), spread).astype(BF16)
        fill(0, even)

    def products(left, offset):
        rows = slice(offset, offset + tile_rows)
        clip = clip_rows[pl.ds(pl.multiple_of(step * 2 * tile_rows + offset, tile_rows), tile_rows), :]
        clip_squared = clip * clip
        for tile in range(s.slots // tile_slots):
            place = slice(tile * width, (tile + 1) * width)
            spots = range(tile * tile_slots, (tile + 1) * tile_slots)
            pieces = [right[:, spot].reshape(s.depth, LANES) for spot in spots]
            joined = jnp.concatenate(pieces, axis=1)
            base_real = recorded[0, rows, place].astype(F32)
            base_imag = recorded[1, rows, place].astype(F32)
            for which, out in enumerate((out_first, out_second)):
                first = 2 * which * tile_rows
                product = dot(left[first : first + 2 * tile_rows], joined)
                real, imag = product[:tile_rows], product[tile_rows:]
                limiter = limited(real, imag, clip, clip_squared)
                out[0, rows, place] = (base_real - real * limiter).astype(BF16)
                out[1, rows, place] = (base_imag - imag * limiter).astype(BF16)

    fill(2 * step + 1, odd)
    products(even, 0)
    fill(jnp.minimum(2 * step + 2, 2 * steps - 1), even)
    products(odd, tile_rows)


def update(recorded, clip_level, left_blocks, filtered, s):
    tile_rows, tile_slots = ROW_BLOCK // 2, 2
    places = s.n_src * s.n_rcv
    anywhere = pl.BlockSpec(memory_space=pl.ANY)
    block = pl.BlockSpec((2, 2 * tile_rows, s.cols), lambda i: (0, i, 0))
    return pl.pallas_call(
        functools.partial(update_kernel, s, tile_rows, tile_slots),
        grid=(s.rows // (2 * tile_rows),),
        in_specs=[block, pl.BlockSpec(memory_space=pltpu.VMEM)]
        + [anywhere] * (len(left_blocks) + len(filtered)),
        out_specs=[block, block],
        out_shape=[jax.ShapeDtypeStruct(recorded.shape, BF16)] * 2,
        scratch_shapes=[
            pltpu.VMEM((places, s.slots + s.halves, 2 * s.own, LANES), BF16),
            pltpu.VMEM((s.depth, s.depth), BF16),
            pltpu.VMEM((4 * tile_rows, s.depth), BF16),
            pltpu.VMEM((4 * tile_rows, s.depth), BF16),
            pltpu.SemaphoreType.DMA((places,)),
            pltpu.SemaphoreType.DMA((len(left_blocks),)),
            pltpu.VMEM((len(left_blocks), s.rows, LANES), BF16),
        ],
        compiler_params=pltpu.CompilerParams(vmem_limit_bytes=VMEM_BYTES),
        cost_estimate=pl.CostEstimate(
            flops=32 * s.rows * s.cols * PANEL,
            bytes_accessed=12 * s.rows * s.cols,
            transcendentals=0,
        ),
        name="update",
    )(recorded, clip_level[:, None], *left_blocks, *filtered)


def rotate(block, ahead, count):
    pairs = [(at, (at + ahead) % count) for at in range(count)]
    return lax.ppermute(block, "rcv", pairs)


def exchange(blocks, count):
    return [blocks[0]] + [rotate(blocks[k], k, count) for k in range(1, count)]


def route(at, place, count):
    if count != 4:
        return (at - place) % count
    return {0: 0, 1: 1, 2: 2, 3: 4}[at ^ place] if at ^ place != 3 or abs(at - place) == 3 else 3


def gather_both(block, pieces, s):
    def swap(held, axis, count, step):
        return lax.ppermute(held, axis, [(at, at ^ step) for at in range(count)])

    line = s.n_rcv == 4
    if line:
        far, outer = swap(block, "rcv", 4, 2), swap(block, "rcv", 4, 1)
        left = (far, outer)
    else:
        left = tuple(exchange([block] * s.n_rcv, s.n_rcv)[1:])
    chips = {step: swap(pieces, "src", s.n_src, step) for step in range(2, s.n_src, 2)}
    block, left, chips, pieces = lax.optimization_barrier((block, left, chips, pieces))
    chips[0] = pieces
    if line:
        far, outer = left
        ends = lax.ppermute(far, "rcv", [(1, 0), (2, 3)])
        middle = lax.ppermute(block, "rcv", [(1, 2), (2, 1)])
        left = (outer, far, middle, ends)
    count = s.n_src // 2
    halves = [range(0, count // 2), range(count // 2, count)]
    same = [jnp.stack([chips[2 * at] for at in half]) for half in halves]
    other = [swap(half, "src", s.n_src, 1) for half in same]
    return (block,) + left, same + other


def per_device(recorded, obliquity, clip_level):
    s = Sizes(recorded, lax.axis_size("src"), lax.axis_size("rcv"))
    if not s.fits():
        return plain_device(recorded, obliquity, clip_level)
    blocks = s.rows // PICK_ROWS
    picked_rows = pick_rows(recorded, s)
    moved = exchange(picked_rows, s.n_rcv)
    early = pick_columns(recorded, 0, EARLY, s.cols // 2, picked_rows[0], s)
    rows = filter_rows(moved, obliquity, early, s)[0]
    returned = exchange(rows, s.n_rcv)
    late = pick_columns(recorded, EARLY, blocks - EARLY, s.cols // 4, rows[0], s)
    pieces, columns = lax.optimization_barrier(
        (jnp.stack(returned), jnp.concatenate([early, late]))
    )
    left_blocks, filtered = gather_both(columns, pieces, s)
    return update(recorded, clip_level, left_blocks, filtered, s)


def solution(mesh):
    return jax.shard_map(
        per_device,
        mesh=mesh,
        in_specs=(P(None, "src", "rcv"), P(), P("src")),
        out_specs=(P(None, "src", "rcv"), P(None, "src", "rcv")),
        check_vma=False,
    )
```
